32 devices in a mesh: groups: 2 (over y), tp: 4 (over z), sub: 4 (over x, core).
Axes of the slice: x: 2, y: 2, z: 4, core: 2. Of those that a mesh axis runs over, the one named last changes fastest.
Arguments:
- queries: bfloat16 [8, 64, 16384], P(('groups', 'sub'), None, 'tp'), parts along dimension 0, may hold values from -128 to 128
- block_kv: bfloat16 [8, 64, 2, 512], P(('groups', 'sub'), None, None, 'tp'), parts along dimension 0, may hold values from -64 to 64
- cache_kv: bfloat16 [8, 2, 4, 1024, 128], P(('groups', 'sub'), None, 'tp'), parts along dimension 0, may hold values from -64 to 64
- prefix_len: int32 [8], P(('groups', 'sub')), parts along dimension 0, may hold values from 128 to 1024, as said below
- residual: bfloat16 [512, 16384], P(('groups', 'tp'), 'sub'), parts along dimension 0, may hold values from -3 to 3
- out_weight: bfloat16 [16384, 16384], P('tp', 'sub'), may hold values from -0.375 to 0.375
Outputs:
- mixed: bfloat16 [512, 16384], P('groups', 'sub'), parts along dimension 0
The draws below stay inside these ranges and needn't reach their ends.
There are 2 independent parts, one for each index of `groups`. The reference program is written for one: setup_inputs(seed, part) draws one part's arguments, and reference() takes and returns one part's arrays. A program takes and returns all parts, laid end to end along the dimension named above; an argument that names none is the same for every part. Nothing has to cross between parts.
Inputs may be any that keep to these rules, and one draw needn't show every extreme that they name: `prefix_len`: cache slots below a request's length hold its prefix; some request has exactly 1024.
All inputs are finite; a program needn't handle non-finite values.
Results may differ from the reference program's by a relative error of at most 0.0062.
Values may be sent and summed in bfloat16 or wider, within the bound.
A program may use at most 128 MiB of HBM per device.

```python
import jax
import jax.numpy as jnp
from jax import lax

D = 16384
HEADS = 128
HD = 128
BLOCK = 64
CAP = 1024
KVR = 4
REQUESTS = 4
TOKENS = 256


def draw_queries(key, part):
    key = jax.random.fold_in(key, 11)
    values = jnp.clip(jax.random.normal(key, (REQUESTS, BLOCK, HEADS * HD), jnp.float32), -6.0, 6.0)
    return values.astype(jnp.bfloat16)


def draw_block_kv(key, part):
    key = jax.random.fold_in(key, 12)
    values = jnp.clip(jax.random.normal(key, (REQUESTS, BLOCK, 2, KVR * HD), jnp.float32), -6.0, 6.0)
    values = values * jnp.array([1.0, 2.0], jnp.float32).reshape(1, 1, 2, 1)
    return values.astype(jnp.bfloat16)


def draw_cache_kv(key, part):
    key = jax.random.fold_in(key, 13)
    values = jnp.clip(jax.random.normal(key, (REQUESTS, 2, KVR, CAP, HD), jnp.float32), -6.0, 6.0)
    values = values * jnp.array([1.0, 2.0], jnp.float32).reshape(1, 2, 1, 1, 1)
    return values.astype(jnp.bfloat16)


def draw_prefix_len(key, part):
    key = jax.random.fold_in(key, 14)
    lengths = jax.random.randint(key, (REQUESTS,), CAP // 8, CAP + 1)
    longest = jax.random.randint(jax.random.fold_in(key, 1), (), 0, REQUESTS)
    return jnp.where(jnp.arange(REQUESTS) == longest, CAP, lengths).astype(jnp.int32)


def block_scale(rng, shape, split, least, top_value):
    level, own = 1.0, jax.random.fold_in(rng, 6)
    for dim, parts in split:
        steps = jnp.exp(jax.random.uniform(jax.random.fold_in(own, dim), (parts,), jnp.float32, least / len(split), top_value / len(split)))
        level = level * jnp.repeat(steps, shape[dim] // parts).reshape([-1 if axis == dim else 1 for axis in range(len(shape))])
    return level


def scatter_about(own_key, dims, scale, limit, split=(), held_as=jnp.bfloat16):
    values = scale * jax.random.normal(own_key, dims, jnp.float32)
    if split:
        values = values * block_scale(own_key, dims, split, -0.22, 0.18)
    return jnp.clip(values, -limit, limit).astype(held_as)


def setup_inputs(seed: int = 0, part: int = 0) -> dict:
    arg_keys = jax.random.split(jax.random.key(seed), 7)
    own_keys = jax.random.split(jax.random.fold_in(arg_keys[6], part), 7)
    queries = draw_queries(jax.random.fold_in(jax.random.fold_in(arg_keys[6], part), 71), part)
    block_kv = draw_block_kv(jax.random.fold_in(jax.random.fold_in(arg_keys[6], part), 71), part)
    cache_kv = draw_cache_kv(jax.random.fold_in(jax.random.fold_in(arg_keys[6], part), 71), part)
    prefix_len = draw_prefix_len(jax.random.fold_in(jax.random.fold_in(arg_keys[6], part), 71), part)
    residual = scatter_about(own_keys[4], (TOKENS, D), 0.5, 3.0, ((0, 4), (1, 4)))
    out_weight = scatter_about(arg_keys[5], (HEADS * HD, D), (2 * HD) ** -0.5, 0.375, ((0, 4), (1, 4)))
    return dict(queries=queries, block_kv=block_kv, cache_kv=cache_kv, prefix_len=prefix_len, residual=residual, out_weight=out_weight)


def attend_one(query, block, cache, length):
    steps = query.shape[0]
    group = HEADS // KVR
    heads_q = query.astype(jnp.float32).reshape(steps, KVR, group, HD)
    block_keys = block[:, 0].astype(jnp.float32).reshape(steps, KVR, HD)
    block_vals = block[:, 1].astype(jnp.float32).reshape(steps, KVR, HD)
    cache_keys = cache[0].astype(jnp.float32)
    cache_vals = cache[1].astype(jnp.float32)
    scale = HD ** -0.5
    cached = jnp.einsum("ckgd,kpd->kgcp", heads_q, cache_keys) * scale
    valid = jnp.arange(CAP) < length
    cached = jnp.where(valid[None, None, None, :], cached, -jnp.inf)
    local = jnp.einsum("ckgd,ekd->kgce", heads_q, block_keys) * scale
    causal = jnp.arange(steps)[:, None] >= jnp.arange(steps)[None, :]
    local = jnp.where(causal[None, None], local, -jnp.inf)
    top = jnp.maximum(jnp.max(cached, axis=-1), jnp.max(local, axis=-1))
    exp_cached = jnp.exp(cached - top[..., None])
    exp_local = jnp.exp(local - top[..., None])
    total = jnp.sum(exp_cached, axis=-1) + jnp.sum(exp_local, axis=-1)
    w_cached = lax.optimization_barrier((exp_cached / total[..., None]).astype(jnp.bfloat16)).astype(jnp.float32)
    w_local = lax.optimization_barrier((exp_local / total[..., None]).astype(jnp.bfloat16)).astype(jnp.float32)
    result = jnp.einsum("kgcp,kpd->ckgd", w_cached, cache_vals) + jnp.einsum("kgce,ekd->ckgd", w_local, block_vals)
    return result.reshape(steps, HEADS * HD).astype(jnp.bfloat16)


def reference(queries, block_kv, cache_kv, prefix_len, residual, out_weight):
    attended = lax.map(lambda item: attend_one(item[0], item[1], item[2], item[3]), (queries, block_kv, cache_kv, prefix_len))
    attended = attended.reshape(TOKENS, HEADS * HD)
    width = HEADS * HD // KVR
    rank_rows = attended.reshape(TOKENS, KVR, width).transpose(1, 0, 2)
    rank_weights = out_weight.reshape(KVR, width, D)

    def add_rank(total, pair):
        partial_value = jnp.dot(pair[0], pair[1], preferred_element_type=jnp.float32)
        rounded = lax.optimization_barrier(partial_value.astype(jnp.bfloat16)).astype(jnp.float32)
        return total + rounded, None

    summed = lax.scan(add_rank, jnp.zeros((TOKENS, D), jnp.float32), (rank_rows, rank_weights))[0]
    return (residual.astype(jnp.float32) + summed).astype(jnp.bfloat16)
```

```python
import jax
import jax.numpy as jnp
from jax import lax
from jax.experimental import pallas as pl
from jax.experimental.pallas import tpu as pltpu
from jax.sharding import PartitionSpec as P

HD = 128


def attend_local(queries, block_kv, cache_kv, prefix_len):
    req_count, steps, width = queries.shape
    group = width // HD
    capacity = cache_kv.shape[3]
    heads_q = queries.reshape(req_count, steps, group, HD)
    block_keys = block_kv[:, :, 0, :]
    block_vals = block_kv[:, :, 1, :]
    cache_keys = cache_kv[:, 0, 0]
    cache_vals = cache_kv[:, 1, 0]
    scale = HD ** (-0.5)
    cached = (
        jnp.einsum("rcgd,rpd->rgcp", heads_q, cache_keys, preferred_element_type=jnp.float32)
        * scale
    )
    valid = jnp.arange(capacity)[None, :] < prefix_len[:, None]
    cached = jnp.where(valid[:, None, None, :], cached, -jnp.inf)
    local = (
        jnp.einsum("rcgd,red->rgce", heads_q, block_keys, preferred_element_type=jnp.float32)
        * scale
    )
    causal = jnp.arange(steps)[:, None] >= jnp.arange(steps)[None, :]
    local = jnp.where(causal[None, None], local, -jnp.inf)
    top = jnp.maximum(jnp.max(cached, axis=-1), jnp.max(local, axis=-1))
    exp_cached = jnp.exp(cached - top[..., None])
    exp_local = jnp.exp(local - top[..., None])
    total = jnp.sum(exp_cached, axis=-1) + jnp.sum(exp_local, axis=-1)
    w_cached = (exp_cached / total[..., None]).astype(jnp.bfloat16)
    w_local = (exp_local / total[..., None]).astype(jnp.bfloat16)
    result = jnp.einsum("rgcp,rpd->rcgd", w_cached, cache_vals, preferred_element_type=jnp.float32)
    result = result + jnp.einsum(
        "rgce,red->rcgd", w_local, block_vals, preferred_element_type=jnp.float32
    )
    return result.reshape(req_count * steps, width).astype(jnp.bfloat16)


def shards(queries, block_kv, cache_kv, prefix_len, residual, out_weight):
    attended = attend_local(queries, block_kv, cache_kv, prefix_len)
    partial_value = jnp.dot(
        lax.all_gather(attended, "sub", axis=0, tiled=True),
        out_weight,
        preferred_element_type=jnp.float32,
    ).astype(jnp.bfloat16)
    terms = lax.optimization_barrier(partial_value).astype(jnp.float32)
    summed = lax.psum_scatter(terms, "tp", scatter_dimension=0, tiled=True)
    stream_rows = (residual.astype(jnp.float32) + summed).astype(jnp.bfloat16)
    return lax.all_gather(stream_rows, "tp", axis=0, tiled=True)


TP_LINE, SUB_RING = 4, 4
TILE, LAG = 512, 2
MESH = pl.DeviceIdType.MESH


def mix_kernel(att, res, w, out, rows, wv, acc, snd, rin, xin, tot, wsem, gsem, grcv, asem, esem, isem, tsem, tend, osem):
    t, s = lax.axis_index("tp"), lax.axis_index("sub")
    core, chip = s % 2, s // 2
    sibling, across = chip * 2 + 1 - core, (1 - chip) * 2 + core
    edge = (t == 0) | (t == TP_LINE - 1)
    inner = (t == 1) | (t == 2)
    side = t // 2
    inward = 1 + side
    outward = side * 3
    opposite = 3 - t
    block = att.shape[0]
    tiles = wv.shape[0]
    chunks = 2 * tiles

    def load(j):
        return pltpu.make_async_copy(w.at[:, pl.ds(pl.multiple_of(j * TILE, TILE), TILE)], wv.at[j], wsem.at[j])

    def start_load(j, carry):
        load(j).start()
        return carry

    lax.fori_loop(0, tiles, start_load, 0)

    barrier = pltpu.get_barrier_semaphore()
    for peer in (sibling, across):
        pl.semaphore_signal(barrier, inc=1, device_id={"sub": peer}, device_id_type=MESH)

    @pl.when(edge)
    def _():
        pl.semaphore_signal(barrier, inc=1, device_id={"tp": inward}, device_id_type=MESH)
        pl.semaphore_wait(barrier, 3)

    @pl.when(inner)
    def _():
        pl.semaphore_signal(barrier, inc=1, device_id={"tp": outward}, device_id_type=MESH)
        pl.semaphore_signal(barrier, inc=1, device_id={"tp": opposite}, device_id_type=MESH)
        pl.semaphore_wait(barrier, 4)

    mine = pl.ds(pl.multiple_of(core * block, block), block)

    def gather(src, slot, n, peer):
        return pltpu.make_async_remote_copy(
            src_ref=src, dst_ref=rows.at[slot, mine], send_sem=gsem.at[n], recv_sem=grcv.at[n],
            device_id={"sub": peer}, device_id_type=MESH,
        )

    to_sibling = gather(att, 0, 0, sibling)
    to_across = gather(att, 1, 1, across)
    forward = gather(rows.at[1, mine], 1, 2, sibling)
    to_across.start()
    to_sibling.start()
    rows[0, mine, :] = att[...]
    to_sibling.wait_recv()

    def send(src, dst, n, out_sem, in_sem, peer):
        return pltpu.make_async_remote_copy(
            src_ref=src.at[n], dst_ref=dst.at[n], send_sem=out_sem.at[n], recv_sem=in_sem.at[n],
            device_id={"tp": peer}, device_id_type=MESH,
        )

    def from_edge(n):
        return send(snd, rin, n, asem, esem, inward)

    def to_opposite(n):
        return send(snd, xin, n, asem, isem, opposite)

    def to_edge(n):
        return send(tot, tot, n, tsem, tend, outward)

    def store(n):
        phase, j = n // tiles, n % tiles
        part = chip + phase - 2 * chip * phase
        return pltpu.make_async_copy(
            tot.at[n],
            out.at[
                pl.ds(pl.multiple_of(part * 2 * block, 2 * block), 2 * block),
                pl.ds(pl.multiple_of(j * TILE, TILE), TILE),
            ],
            osem.at[n],
        )

    def finish(n):
        to_opposite(n).wait_recv()
        total = snd[n].astype(jnp.float32) + xin[n].astype(jnp.float32)
        tot[n] = total.astype(tot.dtype)
        to_edge(n).start()
        store(n).start()

    def step(n, carry):
        phase, j = n // tiles, n % tiles
        part = chip + phase - 2 * chip * phase

        @pl.when(phase == 0)
        def _():
            load(j).wait()

        @pl.when(n == tiles // 2)
        def _():
            to_across.wait_recv()
            forward.start()

        @pl.when(n == tiles)
        def _():
            forward.wait_recv()

        acc[...] = jnp.dot(rows[phase], wv[j], preferred_element_type=jnp.float32)

        @pl.when(side == part)
        def _():
            at = pl.ds(pl.multiple_of((t % 2) * block, block), block)
            acc[at, :] += res[:, pl.ds(pl.multiple_of(j * TILE, TILE), TILE)].astype(jnp.float32)

        @pl.when(edge)
        def _():
            snd[n] = acc[...].astype(snd.dtype)
            from_edge(n).start()

        @pl.when(inner)
        def _():
            from_edge(n).wait_recv()
            snd[n] = (acc[...] + rin[n].astype(jnp.float32)).astype(snd.dtype)
            to_opposite(n).start()

        @pl.when(inner & (n >= LAG))
        def _():
            finish(n - LAG)

        return carry

    lax.fori_loop(0, chunks, step, 0)

    @pl.when(inner)
    def _():
        def rest(n, carry):
            finish(n)
            return carry

        lax.fori_loop(chunks - LAG, chunks, rest, 0)

        def drain(n, carry):
            to_opposite(n).wait_send()
            to_edge(n).wait_send()
            store(n).wait()
            return carry

        lax.fori_loop(0, chunks, drain, 0)

    @pl.when(edge)
    def _():
        def take(n, carry):
            to_edge(n).wait_recv()
            store(n).start()
            return carry

        lax.fori_loop(0, chunks, take, 0)

        def drain(n, carry):
            from_edge(n).wait_send()
            store(n).wait()
            return carry

        lax.fori_loop(0, chunks, drain, 0)

    to_sibling.wait_send()
    to_across.wait_send()
    forward.wait_send()


def mix(attended, residual, out_weight):
    block, depth = attended.shape
    width = out_weight.shape[1]
    tiles = width // TILE
    chunks = 2 * tiles
    dma = pltpu.SemaphoreType.DMA
    chunk_buffer = pltpu.VMEM((chunks, 2 * block, TILE), jnp.bfloat16)
    return pl.pallas_call(
        mix_kernel,
        out_shape=jax.ShapeDtypeStruct((4 * block, width), jnp.bfloat16),
        in_specs=[
            pl.BlockSpec(memory_space=pltpu.VMEM),
            pl.BlockSpec(memory_space=pltpu.VMEM),
            pl.BlockSpec(memory_space=pl.ANY),
        ],
        out_specs=pl.BlockSpec(memory_space=pl.ANY),
        scratch_shapes=[
            pltpu.VMEM((2, 2 * block, depth), jnp.bfloat16),
            pltpu.VMEM((tiles, depth, TILE), jnp.bfloat16),
            pltpu.VMEM((2 * block, TILE), jnp.float32),
            chunk_buffer,
            chunk_buffer,
            chunk_buffer,
            chunk_buffer,
            dma((tiles,)),
            dma((3,)),
            dma((3,)),
            dma((chunks,)),
            dma((chunks,)),
            dma((chunks,)),
            dma((chunks,)),
            dma((chunks,)),
            dma((chunks,)),
        ],
        compiler_params=pltpu.CompilerParams(
            collective_id=0, has_side_effects=True, vmem_limit_bytes=52 * 1024 * 1024
        ),
    )(attended, residual, out_weight)


def line_shards(queries, block_kv, cache_kv, prefix_len, residual, out_weight):
    return mix(attend_local(queries, block_kv, cache_kv, prefix_len), residual, out_weight)


def solution(mesh):
    in_specs = (
        P(("groups", "sub"), None, "tp"),
        P(("groups", "sub"), None, None, "tp"),
        P(("groups", "sub"), None, "tp", None, None),
        P(("groups", "sub")),
        P(("groups", "tp"), "sub"),
        P("tp", "sub"),
    )
    out_specs = P("groups", "sub")
    fits = mesh.shape["tp"] == TP_LINE and mesh.shape["sub"] == SUB_RING
    body = line_shards if fits else shards
    return jax.shard_map(body, mesh=mesh, in_specs=in_specs, out_specs=out_specs, check_vma=False)
```

```python
import jax
import jax.numpy as jnp
from jax import lax
from jax.experimental import pallas as pl
from jax.experimental.pallas import tpu as pltpu
from jax.sharding import PartitionSpec as P

HD = 128


def attend_local(queries, block_kv, cache_kv, prefix_len):
    req_count, steps, width = queries.shape
    group = width // HD
    capacity = cache_kv.shape[3]
    heads_q = queries.reshape(req_count, steps, group, HD)
    block_keys = block_kv[:, :, 0, :]
    block_vals = block_kv[:, :, 1, :]
    cache_keys = cache_kv[:, 0, 0]
    cache_vals = cache_kv[:, 1, 0]
    scale = HD ** (-0.5)
    cached = (
        jnp.einsum("rcgd,rpd->rgcp", heads_q, cache_keys, preferred_element_type=jnp.float32)
        * scale
    )
    valid = jnp.arange(capacity)[None, :] < prefix_len[:, None]
    cached = jnp.where(valid[:, None, None, :], cached, -jnp.inf)
    local = (
        jnp.einsum("rcgd,red->rgce", heads_q, block_keys, preferred_element_type=jnp.float32)
        * scale
    )
    causal = jnp.arange(steps)[:, None] >= jnp.arange(steps)[None, :]
    local = jnp.where(causal[None, None], local, -jnp.inf)
    top = jnp.maximum(jnp.max(cached, axis=-1), jnp.max(local, axis=-1))
    exp_cached = jnp.exp(cached - top[..., None])
    exp_local = jnp.exp(local - top[..., None])
    total = jnp.sum(exp_cached, axis=-1) + jnp.sum(exp_local, axis=-1)
    w_cached = (exp_cached / total[..., None]).astype(jnp.bfloat16)
    w_local = (exp_local / total[..., None]).astype(jnp.bfloat16)
    result = jnp.einsum("rgcp,rpd->rcgd", w_cached, cache_vals, preferred_element_type=jnp.float32)
    result = result + jnp.einsum(
        "rgce,red->rcgd", w_local, block_vals, preferred_element_type=jnp.float32
    )
    return result.reshape(req_count * steps, width).astype(jnp.bfloat16)


def shards(queries, block_kv, cache_kv, prefix_len, residual, out_weight):
    attended = attend_local(queries, block_kv, cache_kv, prefix_len)
    partial_value = jnp.dot(
        lax.all_gather(attended, "sub", axis=0, tiled=True),
        out_weight,
        preferred_element_type=jnp.float32,
    ).astype(jnp.bfloat16)
    terms = lax.optimization_barrier(partial_value).astype(jnp.float32)
    summed = lax.psum_scatter(terms, "tp", scatter_dimension=0, tiled=True)
    stream_rows = (residual.astype(jnp.float32) + summed).astype(jnp.bfloat16)
    return lax.all_gather(stream_rows, "tp", axis=0, tiled=True)


TP_LINE, SUB_RING = 4, 4
TILE, LAG = 256, 2
HEADS_AT_ONCE = 4
LOG2E = 1.4426950408889634
MESH = pl.DeviceIdType.MESH


def mix_kernel(
    lens, queries, new_kv, cache, res, w, out, qv, bv, cv, rows, wv, acc, snd, rin, xin, tot,
    qsem, wsem, psem, prcv, gsem, grcv, asem, esem, isem, tsem, tend, osem,
):
    t, s = lax.axis_index("tp"), lax.axis_index("sub")
    core, chip = s % 2, s // 2
    sibling, across = chip * 2 + 1 - core, (1 - chip) * 2 + core
    edge = (t == 0) | (t == TP_LINE - 1)
    inner = (t == 1) | (t == 2)
    side = t // 2
    inward = 1 + side
    outward = side * 3
    opposite = 3 - t
    block = res.shape[0]
    span = HEADS_AT_ONCE * HD
    groups = qv.shape[1] // span
    tiles = wv.shape[0]
    chunks = 2 * tiles

    def load(j):
        return pltpu.make_async_copy(w.at[:, pl.ds(pl.multiple_of(j * TILE, TILE), TILE)], wv.at[j], wsem.at[j])

    def start_load(j, carry):
        load(j).start()
        return carry

    first = [
        pltpu.make_async_copy(src, dst, qsem.at[n])
        for n, (src, dst) in enumerate(((queries, qv), (new_kv, bv), (cache, cv)))
    ]
    for copy in first:
        copy.start()
    lax.fori_loop(0, tiles, start_load, 0)

    barrier = pltpu.get_barrier_semaphore()
    for peer in (sibling, across):
        pl.semaphore_signal(barrier, inc=1, device_id={"sub": peer}, device_id_type=MESH)

    @pl.when(edge)
    def _():
        pl.semaphore_signal(barrier, inc=1, device_id={"tp": inward}, device_id_type=MESH)

    @pl.when(inner)
    def _():
        pl.semaphore_signal(barrier, inc=1, device_id={"tp": outward}, device_id_type=MESH)
        pl.semaphore_signal(barrier, inc=1, device_id={"tp": opposite}, device_id_type=MESH)

    mine = pl.ds(pl.multiple_of(core * block, block), block)

    def piece(n):
        part_of_row = rows.at[0, mine, pl.ds(pl.multiple_of(n * span, span), span)]
        return pltpu.make_async_remote_copy(
            src_ref=part_of_row, dst_ref=part_of_row, send_sem=psem.at[n], recv_sem=prcv.at[n],
            device_id={"sub": sibling}, device_id_type=MESH,
        )

    def gather(slot, n, peer):
        return pltpu.make_async_remote_copy(
            src_ref=rows.at[slot, mine], dst_ref=rows.at[1, mine], send_sem=gsem.at[n], recv_sem=grcv.at[n],
            device_id={"sub": peer}, device_id_type=MESH,
        )

    to_across = gather(0, 0, across)
    forward = gather(1, 1, sibling)

    for copy in first:
        copy.wait()
    capacity = cv.shape[1]
    held = lax.broadcasted_iota(jnp.int32, (1, capacity), 1) < lens[0]
    bias = jnp.where(held, 0.0, -jnp.inf).astype(jnp.float32)
    many = HEADS_AT_ONCE * block
    token = lax.rem(lax.broadcasted_iota(jnp.int32, (many, block), 0), block)
    causal = token >= lax.broadcasted_iota(jnp.int32, (many, block), 1)
    factor = HD ** (-0.5) * LOG2E
    last = (((1,), (1,)), ((), ()))

    def attend(n, carry):
        wide = qv[:, pl.ds(pl.multiple_of(n * span, span), span)]
        q = jnp.concatenate([wide[:, i * HD : (i + 1) * HD] for i in range(HEADS_AT_ONCE)], axis=0)
        old = lax.dot_general(q, cv[0], last, preferred_element_type=jnp.float32) + bias
        new = lax.dot_general(q, bv[:, :HD], last, preferred_element_type=jnp.float32)
        new = jnp.where(causal, new, -jnp.inf)
        top = jnp.maximum(jnp.max(old, axis=1, keepdims=True), jnp.max(new, axis=1, keepdims=True))
        old = jnp.exp2((old - top) * factor)
        new = jnp.exp2((new - top) * factor)
        part = 1.0 / (jnp.sum(old, axis=1, keepdims=True) + jnp.sum(new, axis=1, keepdims=True))
        got = jnp.dot((old * part).astype(jnp.bfloat16), cv[1], preferred_element_type=jnp.float32)
        got += jnp.dot((new * part).astype(jnp.bfloat16), bv[:, HD:], preferred_element_type=jnp.float32)
        for i in range(HEADS_AT_ONCE):
            at = pl.ds(pl.multiple_of(n * span + i * HD, HD), HD)
            rows[0, mine, at] = got[i * block : (i + 1) * block].astype(jnp.bfloat16)

        @pl.when(n == 0)
        def _():
            pl.semaphore_wait(barrier, jnp.where(edge, 3, 4))

        piece(n).start()
        return carry

    lax.fori_loop(0, groups, attend, 0)
    to_across.start()

    def take_piece(n, carry):
        piece(n).wait_recv()
        return carry

    lax.fori_loop(0, groups, take_piece, 0)

    def send(src, dst, n, out_sem, in_sem, peer):
        return pltpu.make_async_remote_copy(
            src_ref=src.at[n], dst_ref=dst.at[n], send_sem=out_sem.at[n], recv_sem=in_sem.at[n],
            device_id={"tp": peer}, device_id_type=MESH,
        )

    def from_edge(n):
        return send(snd, rin, n, asem, esem, inward)

    def to_opposite(n):
        return send(snd, xin, n, asem, isem, opposite)

    def to_edge(n):
        return send(tot, tot, n, tsem, tend, outward)

    def store(n):
        phase, j = n // tiles, n % tiles
        part = chip + phase - 2 * chip * phase
        return pltpu.make_async_copy(
            tot.at[n],
            out.at[
                pl.ds(pl.multiple_of(part * 2 * block, 2 * block), 2 * block),
                pl.ds(pl.multiple_of(j * TILE, TILE), TILE),
            ],
            osem.at[n],
        )

    def finish(n):
        to_opposite(n).wait_recv()
        total = snd[n].astype(jnp.float32) + xin[n].astype(jnp.float32)
        tot[n] = total.astype(tot.dtype)
        to_edge(n).start()
        store(n).start()

    def step(n, carry):
        phase, j = n // tiles, n % tiles
        part = chip + phase - 2 * chip * phase

        @pl.when(phase == 0)
        def _():
            load(j).wait()

        @pl.when(n == tiles // 2)
        def _():
            to_across.wait_recv()
            forward.start()

        @pl.when(n == tiles)
        def _():
            forward.wait_recv()

        acc[...] = jnp.dot(rows[phase], wv[j], preferred_element_type=jnp.float32)

        @pl.when(side == part)
        def _():
            at = pl.ds(pl.multiple_of((t % 2) * block, block), block)
            acc[at, :] += res[:, pl.ds(pl.multiple_of(j * TILE, TILE), TILE)].astype(jnp.float32)

        @pl.when(edge)
        def _():
            snd[n] = acc[...].astype(snd.dtype)
            from_edge(n).start()

        @pl.when(inner)
        def _():
            from_edge(n).wait_recv()
            snd[n] = (acc[...] + rin[n].astype(jnp.float32)).astype(snd.dtype)
            to_opposite(n).start()

        @pl.when(inner & (n >= LAG))
        def _():
            finish(n - LAG)

        return carry

    lax.fori_loop(0, chunks, step, 0)

    @pl.when(inner)
    def _():
        def rest(n, carry):
            finish(n)
            return carry

        lax.fori_loop(chunks - LAG, chunks, rest, 0)

        def drain(n, carry):
            to_opposite(n).wait_send()
            to_edge(n).wait_send()
            store(n).wait()
            return carry

        lax.fori_loop(0, chunks, drain, 0)

    @pl.when(edge)
    def _():
        def take(n, carry):
            to_edge(n).wait_recv()
            store(n).start()
            return carry

        lax.fori_loop(0, chunks, take, 0)

        def drain(n, carry):
            from_edge(n).wait_send()
            store(n).wait()
            return carry

        lax.fori_loop(0, chunks, drain, 0)

    def drain_piece(n, carry):
        piece(n).wait_send()
        return carry

    lax.fori_loop(0, groups, drain_piece, 0)
    to_across.wait_send()
    forward.wait_send()


def line_shards(queries, block_kv, cache_kv, prefix_len, residual, out_weight):
    block, depth = queries.shape[1:]
    width = out_weight.shape[1]
    tiles = width // TILE
    chunks = 2 * tiles
    groups = depth // (HEADS_AT_ONCE * HD)
    dma = pltpu.SemaphoreType.DMA
    chunk_buffer = pltpu.VMEM((chunks, 2 * block, TILE), jnp.bfloat16)
    anywhere = pl.BlockSpec(memory_space=pl.ANY)
    return pl.pallas_call(
        mix_kernel,
        out_shape=jax.ShapeDtypeStruct((4 * block, width), jnp.bfloat16),
        in_specs=[
            pl.BlockSpec(memory_space=pltpu.SMEM),
            anywhere,
            anywhere,
            anywhere,
            pl.BlockSpec(memory_space=pltpu.VMEM),
            anywhere,
        ],
        out_specs=anywhere,
        scratch_shapes=[
            pltpu.VMEM((block, depth), jnp.bfloat16),
            pltpu.VMEM((block, 2 * HD), jnp.bfloat16),
            pltpu.VMEM((2,) + cache_kv.shape[3:], jnp.bfloat16),
            pltpu.VMEM((2, 2 * block, depth), jnp.bfloat16),
            pltpu.VMEM((tiles, depth, TILE), jnp.bfloat16),
            pltpu.VMEM((2 * block, TILE), jnp.float32),
            chunk_buffer,
            chunk_buffer,
            chunk_buffer,
            chunk_buffer,
            dma((3,)),
            dma((tiles,)),
            dma((groups,)),
            dma((groups,)),
            dma((2,)),
            dma((2,)),
            dma((chunks,)),
            dma((chunks,)),
            dma((chunks,)),
            dma((chunks,)),
            dma((chunks,)),
            dma((chunks,)),
        ],
        compiler_params=pltpu.CompilerParams(
            collective_id=0, has_side_effects=True, vmem_limit_bytes=56 * 1024 * 1024
        ),
    )(
        prefix_len,
        queries.reshape(block, depth),
        block_kv.reshape(block, 2 * HD),
        cache_kv.reshape((2,) + cache_kv.shape[3:]),
        residual,
        out_weight,
    )


def solution(mesh):
    in_specs = (
        P(("groups", "sub"), None, "tp"),
        P(("groups", "sub"), None, None, "tp"),
        P(("groups", "sub"), None, "tp", None, None),
        P(("groups", "sub")),
        P(("groups", "tp"), "sub"),
        P("tp", "sub"),
    )
    out_specs = P("groups", "sub")
    fits = mesh.shape["tp"] == TP_LINE and mesh.shape["sub"] == SUB_RING
    body = line_shards if fits else shards
    return jax.shard_map(body, mesh=mesh, in_specs=in_specs, out_specs=out_specs, check_vma=False)
```

```python
import jax
import jax.numpy as jnp
from jax import lax
from jax.experimental import pallas as pl
from jax.experimental.pallas import tpu as pltpu
from jax.sharding import PartitionSpec as P

HD = 128


def attend_local(queries, block_kv, cache_kv, prefix_len):
    req_count, steps, width = queries.shape
    group = width // HD
    capacity = cache_kv.shape[3]
    heads_q = queries.reshape(req_count, steps, group, HD)
    block_keys = block_kv[:, :, 0, :]
    block_vals = block_kv[:, :, 1, :]
    cache_keys = cache_kv[:, 0, 0]
    cache_vals = cache_kv[:, 1, 0]
    scale = HD ** (-0.5)
    cached = (
        jnp.einsum("rcgd,rpd->rgcp", heads_q, cache_keys, preferred_element_type=jnp.float32)
        * scale
    )
    valid = jnp.arange(capacity)[None, :] < prefix_len[:, None]
    cached = jnp.where(valid[:, None, None, :], cached, -jnp.inf)
    local = (
        jnp.einsum("rcgd,red->rgce", heads_q, block_keys, preferred_element_type=jnp.float32)
        * scale
    )
    causal = jnp.arange(steps)[:, None] >= jnp.arange(steps)[None, :]
    local = jnp.where(causal[None, None], local, -jnp.inf)
    top = jnp.maximum(jnp.max(cached, axis=-1), jnp.max(local, axis=-1))
    exp_cached = jnp.exp(cached - top[..., None])
    exp_local = jnp.exp(local - top[..., None])
    total = jnp.sum(exp_cached, axis=-1) + jnp.sum(exp_local, axis=-1)
    w_cached = (exp_cached / total[..., None]).astype(jnp.bfloat16)
    w_local = (exp_local / total[..., None]).astype(jnp.bfloat16)
    result = jnp.einsum("rgcp,rpd->rcgd", w_cached, cache_vals, preferred_element_type=jnp.float32)
    result = result + jnp.einsum(
        "rgce,red->rcgd", w_local, block_vals, preferred_element_type=jnp.float32
    )
    return result.reshape(req_count * steps, width).astype(jnp.bfloat16)


def shards(queries, block_kv, cache_kv, prefix_len, residual, out_weight):
    attended = attend_local(queries, block_kv, cache_kv, prefix_len)
    partial_value = jnp.dot(
        lax.all_gather(attended, "sub", axis=0, tiled=True),
        out_weight,
        preferred_element_type=jnp.float32,
    ).astype(jnp.bfloat16)
    terms = lax.optimization_barrier(partial_value).astype(jnp.float32)
    summed = lax.psum_scatter(terms, "tp", scatter_dimension=0, tiled=True)
    stream_rows = (residual.astype(jnp.float32) + summed).astype(jnp.bfloat16)
    return lax.all_gather(stream_rows, "tp", axis=0, tiled=True)


TP_LINE, SUB_RING = 4, 4
TILE, LAG = 256, 2
HEADS_AT_ONCE = 8
LOG2E = 1.4426950408889634
MESH = pl.DeviceIdType.MESH


def mix_kernel(
    lens, queries, new_kv, cache, res, w, out, qv, both, bv, cv, rows, wv, acc, snd, rin, xin, tot,
    qsem, wsem, psem, prcv, gsem, grcv, asem, esem, isem, tsem, tend, osem,
):
    t, s = lax.axis_index("tp"), lax.axis_index("sub")
    core, chip = s % 2, s // 2
    sibling, across = chip * 2 + 1 - core, (1 - chip) * 2 + core
    edge = (t == 0) | (t == TP_LINE - 1)
    inner = (t == 1) | (t == 2)
    side = t // 2
    inward = 1 + side
    outward = side * 3
    opposite = 3 - t
    block = res.shape[0]
    span = HEADS_AT_ONCE * HD
    groups = qv.shape[1] // span
    tiles = wv.shape[0]
    chunks = 2 * tiles

    def load(j):
        return pltpu.make_async_copy(w.at[:, pl.ds(pl.multiple_of(j * TILE, TILE), TILE)], wv.at[j], wsem.at[j])

    def start_load(j, carry):
        load(j).start()
        return carry

    first = [
        pltpu.make_async_copy(src, dst, qsem.at[n])
        for n, (src, dst) in enumerate(((queries, qv), (new_kv, both), (cache, cv)))
    ]
    for copy in first:
        copy.start()

    barrier = pltpu.get_barrier_semaphore()
    for peer in (sibling, across):
        pl.semaphore_signal(barrier, inc=1, device_id={"sub": peer}, device_id_type=MESH)

    @pl.when(edge)
    def _():
        pl.semaphore_signal(barrier, inc=1, device_id={"tp": inward}, device_id_type=MESH)

    @pl.when(inner)
    def _():
        pl.semaphore_signal(barrier, inc=1, device_id={"tp": outward}, device_id_type=MESH)
        pl.semaphore_signal(barrier, inc=1, device_id={"tp": opposite}, device_id_type=MESH)

    mine = pl.ds(pl.multiple_of(core * block, block), block)

    def piece(n):
        part_of_row = rows.at[0, mine, pl.ds(pl.multiple_of(n * span, span), span)]
        return pltpu.make_async_remote_copy(
            src_ref=part_of_row, dst_ref=part_of_row, send_sem=psem.at[n], recv_sem=prcv.at[n],
            device_id={"sub": sibling}, device_id_type=MESH,
        )

    def gather(slot, n, peer):
        return pltpu.make_async_remote_copy(
            src_ref=rows.at[slot, mine], dst_ref=rows.at[1, mine], send_sem=gsem.at[n], recv_sem=grcv.at[n],
            device_id={"sub": peer}, device_id_type=MESH,
        )

    to_across = gather(0, 0, across)
    forward = gather(1, 1, sibling)

    for copy in first:
        copy.wait()
    which = lax.broadcasted_iota(jnp.int32, both.shape, 1)
    for i in range(2):
        bv[i] = jnp.sum(jnp.where(which == i, both[...].astype(jnp.float32), 0.0), axis=1).astype(bv.dtype)
    capacity = cv.shape[1]
    held = lax.broadcasted_iota(jnp.int32, (1, capacity), 1) < lens[0]
    bias = jnp.where(held, 0.0, -jnp.inf).astype(jnp.float32)
    many = HEADS_AT_ONCE * block
    token = lax.rem(lax.broadcasted_iota(jnp.int32, (many, block), 0), block)
    causal = token >= lax.broadcasted_iota(jnp.int32, (many, block), 1)
    factor = HD ** (-0.5) * LOG2E
    last = (((1,), (1,)), ((), ()))

    per_group = tiles // groups

    def attend(n, carry):
        lax.fori_loop(n * per_group, (n + 1) * per_group, start_load, 0)
        wide = qv[:, pl.ds(pl.multiple_of(n * span, span), span)]
        q = jnp.concatenate([wide[:, i * HD : (i + 1) * HD] for i in range(HEADS_AT_ONCE)], axis=0)
        old = lax.dot_general(q, cv[0], last, preferred_element_type=jnp.float32) + bias
        new = lax.dot_general(q, bv[0], last, preferred_element_type=jnp.float32)
        new = jnp.where(causal, new, -jnp.inf)
        top = jnp.maximum(jnp.max(old, axis=1, keepdims=True), jnp.max(new, axis=1, keepdims=True))
        old = jnp.exp2((old - top) * factor)
        new = jnp.exp2((new - top) * factor)
        part = 1.0 / (jnp.sum(old, axis=1, keepdims=True) + jnp.sum(new, axis=1, keepdims=True))
        got = jnp.dot((old * part).astype(jnp.bfloat16), cv[1], preferred_element_type=jnp.float32)
        got += jnp.dot((new * part).astype(jnp.bfloat16), bv[1], preferred_element_type=jnp.float32)
        for i in range(HEADS_AT_ONCE):
            at = pl.ds(pl.multiple_of(n * span + i * HD, HD), HD)
            rows[0, mine, at] = got[i * block : (i + 1) * block].astype(jnp.bfloat16)

        @pl.when(n == 0)
        def _():
            pl.semaphore_wait(barrier, jnp.where(edge, 3, 4))

        piece(n).start()
        return carry

    lax.fori_loop(0, groups, attend, 0)
    to_across.start()

    def take_piece(n, carry):
        piece(n).wait_recv()
        return carry

    lax.fori_loop(0, groups, take_piece, 0)

    def send(src, dst, n, out_sem, in_sem, peer):
        return pltpu.make_async_remote_copy(
            src_ref=src.at[n], dst_ref=dst.at[n], send_sem=out_sem.at[n], recv_sem=in_sem.at[n],
            device_id={"tp": peer}, device_id_type=MESH,
        )

    def from_edge(n):
        return send(snd, rin, n, asem, esem, inward)

    def to_opposite(n):
        return send(snd, xin, n, asem, isem, opposite)

    def to_edge(n):
        return send(tot, tot, n, tsem, tend, outward)

    def store(n):
        phase, j = n // tiles, n % tiles
        part = chip + phase - 2 * chip * phase
        return pltpu.make_async_copy(
            tot.at[n],
            out.at[
                pl.ds(pl.multiple_of(part * 2 * block, 2 * block), 2 * block),
                pl.ds(pl.multiple_of(j * TILE, TILE), TILE),
            ],
            osem.at[n],
        )

    def finish(n):
        to_opposite(n).wait_recv()
        total = snd[n].astype(jnp.float32) + xin[n].astype(jnp.float32)
        tot[n] = total.astype(tot.dtype)
        to_edge(n).start()
        store(n).start()

    def step(n, carry):
        phase, j = n // tiles, n % tiles
        part = chip + phase - 2 * chip * phase

        @pl.when(phase == 0)
        def _():
            load(j).wait()

        @pl.when(n == tiles // 2)
        def _():
            to_across.wait_recv()
            forward.start()

        @pl.when(n == tiles)
        def _():
            forward.wait_recv()

        acc[...] = jnp.dot(rows[phase], wv[j], preferred_element_type=jnp.float32)

        @pl.when(side == part)
        def _():
            at = pl.ds(pl.multiple_of((t % 2) * block, block), block)
            acc[at, :] += res[:, pl.ds(pl.multiple_of(j * TILE, TILE), TILE)].astype(jnp.float32)

        @pl.when(edge)
        def _():
            snd[n] = acc[...].astype(snd.dtype)
            from_edge(n).start()

        @pl.when(inner)
        def _():
            from_edge(n).wait_recv()
            snd[n] = (acc[...] + rin[n].astype(jnp.float32)).astype(snd.dtype)
            to_opposite(n).start()

        @pl.when(inner & (n >= LAG))
        def _():
            finish(n - LAG)

        return carry

    lax.fori_loop(0, chunks, step, 0)

    @pl.when(inner)
    def _():
        def rest(n, carry):
            finish(n)
            return carry

        lax.fori_loop(chunks - LAG, chunks, rest, 0)

        def drain(n, carry):
            to_opposite(n).wait_send()
            to_edge(n).wait_send()
            store(n).wait()
            return carry

        lax.fori_loop(0, chunks, drain, 0)

    @pl.when(edge)
    def _():
        def take(n, carry):
            to_edge(n).wait_recv()
            store(n).start()
            return carry

        lax.fori_loop(0, chunks, take, 0)

        def drain(n, carry):
            from_edge(n).wait_send()
            store(n).wait()
            return carry

        lax.fori_loop(0, chunks, drain, 0)

    def drain_piece(n, carry):
        piece(n).wait_send()
        return carry

    lax.fori_loop(0, groups, drain_piece, 0)
    to_across.wait_send()
    forward.wait_send()


def line_shards(queries, block_kv, cache_kv, prefix_len, residual, out_weight):
    block, depth = queries.shape[1:]
    width = out_weight.shape[1]
    tiles = width // TILE
    chunks = 2 * tiles
    groups = depth // (HEADS_AT_ONCE * HD)
    dma = pltpu.SemaphoreType.DMA
    chunk_buffer = pltpu.VMEM((chunks, 2 * block, TILE), jnp.bfloat16)
    anywhere = pl.BlockSpec(memory_space=pl.ANY)
    return pl.pallas_call(
        mix_kernel,
        out_shape=jax.ShapeDtypeStruct((4 * block, width), jnp.bfloat16),
        in_specs=[
            pl.BlockSpec(memory_space=pltpu.SMEM),
            anywhere,
            anywhere,
            anywhere,
            pl.BlockSpec(memory_space=pltpu.VMEM),
            anywhere,
        ],
        out_specs=anywhere,
        scratch_shapes=[
            pltpu.VMEM((block, depth), jnp.bfloat16),
            pltpu.VMEM((block, 2, HD), jnp.bfloat16),
            pltpu.VMEM((2, block, HD), jnp.bfloat16),
            pltpu.VMEM((2,) + cache_kv.shape[3:], jnp.bfloat16),
            pltpu.VMEM((2, 2 * block, depth), jnp.bfloat16),
            pltpu.VMEM((tiles, depth, TILE), jnp.bfloat16),
            pltpu.VMEM((2 * block, TILE), jnp.float32),
            chunk_buffer,
            chunk_buffer,
            chunk_buffer,
            chunk_buffer,
            dma((3,)),
            dma((tiles,)),
            dma((groups,)),
            dma((groups,)),
            dma((2,)),
            dma((2,)),
            dma((chunks,)),
            dma((chunks,)),
            dma((chunks,)),
            dma((chunks,)),
            dma((chunks,)),
            dma((chunks,)),
        ],
        compiler_params=pltpu.CompilerParams(
            collective_id=0, has_side_effects=True, vmem_limit_bytes=56 * 1024 * 1024
        ),
    )(
        prefix_len,
        queries.reshape(block, depth),
        block_kv.reshape(block, 2, HD),
        cache_kv.reshape((2,) + cache_kv.shape[3:]),
        residual,
        out_weight,
    )


def solution(mesh):
    in_specs = (
        P(("groups", "sub"), None, "tp"),
        P(("groups", "sub"), None, None, "tp"),
        P(("groups", "sub"), None, "tp", None, None),
        P(("groups", "sub")),
        P(("groups", "tp"), "sub"),
        P("tp", "sub"),
    )
    out_specs = P("groups", "sub")
    fits = mesh.shape["tp"] == TP_LINE and mesh.shape["sub"] == SUB_RING
    body = line_shards if fits else shards
    return jax.shard_map(body, mesh=mesh, in_specs=in_specs, out_specs=out_specs, check_vma=False)
```
